32 devices in a mesh: lib: 8 (over z, y), lmk: 4 (over x, core).
Axes of the slice: x: 2, y: 2, z: 4, core: 2. Of those that a mesh axis runs over, the one named last changes fastest.
Arguments:
- library_bits: bfloat16 [6144, 2048], P('lib'), may hold values from 0 to 1, as said below
- library_count: int32 [6144], P('lib'), may hold values from 1 to 2048, as said below
- landmark_bits: bfloat16 [8192, 2048], P('lmk'), may hold values from 0 to 1, as said below
- landmark_count: int32 [8192], P('lmk'), may hold values from 1 to 2048, as said below
- inverse_root: bfloat16 [8192, 8192], P('lib', 'lmk'), may hold values from -0.09375 to 0.09375
Outputs:
- features: float32 [6144, 8192], P('lib', 'lmk')
The draws below stay inside these ranges and needn't reach their ends.
Inputs may be any that keep to these rules, and one draw needn't show every extreme that they name: `library_bits`: every entry is 0 or 1; every fingerprint has at least one set bit, one has all 2048 set and one has exactly one. `library_count`: the number of ones in the same row of library_bits. `landmark_bits`: every entry is 0 or 1; every fingerprint has at least one set bit, one has all 2048 set and one has exactly one. `landmark_count`: the number of ones in the same row of landmark_bits.
All inputs are finite; a program needn't handle non-finite values.
Results may differ from the reference program's by a relative error of at most 0.0027.
Values may be sent and summed in bfloat16 or wider, within the bound.
A program may use at most 128 MiB of HBM per device.

```python
import jax
import jax.numpy as jnp
from jax import lax

BITS = 2048
NLM = 8192
NLIB = 6144


def fingerprint(key, rows):
    levels = jax.random.randint(jax.random.fold_in(key, 11), (rows, 1), 5, 996)
    raw = jax.random.randint(jax.random.fold_in(key, 12), (rows, BITS), 0, 1000)
    bits = (raw < levels).astype(jnp.int32)
    place = jax.random.randint(jax.random.fold_in(key, 13), (rows, 1), 0, BITS)
    forced = (jnp.arange(BITS, dtype=jnp.int32)[None, :] == place).astype(jnp.int32)
    row_index = jnp.arange(rows, dtype=jnp.int32)[:, None]
    merged = jnp.maximum(bits, forced)
    merged = jnp.where(row_index == 1, forced, merged)
    merged = jnp.where(row_index == 0, jnp.ones_like(merged), merged)
    return merged


def draw_library_bits(key, part):
    bits = fingerprint(jax.random.fold_in(key, 101), NLIB)
    return bits.astype(jnp.float32).astype(jnp.bfloat16)


def draw_library_count(key, part):
    bits = fingerprint(jax.random.fold_in(key, 101), NLIB)
    return jnp.sum(bits, axis=1).astype(jnp.int32)


def draw_landmark_bits(key, part):
    bits = fingerprint(jax.random.fold_in(key, 202), NLM)
    return bits.astype(jnp.float32).astype(jnp.bfloat16)


def draw_landmark_count(key, part):
    bits = fingerprint(jax.random.fold_in(key, 202), NLM)
    return jnp.sum(bits, axis=1).astype(jnp.int32)


def raised(drawn, own_key, source, target, shards_of, factor):
    def block_of(position):
        return (jnp.arange(drawn.shape[position]) // (drawn.shape[position] // shards_of)).reshape((-1,) + (1,) * (drawn.ndim - 1 - position))

    first = jax.random.permutation(own_key, shards_of)[block_of(target)]
    far = (block_of(target) + shards_of // 2) % shards_of
    return jnp.where((block_of(source) == first) | (block_of(source) == far), factor * drawn, drawn)


def block_levels(rng, extent, cuts, low, largest):
    def one(dim, blocks):
        draws = jax.random.uniform(jax.random.fold_in(jax.random.fold_in(rng, 6), dim), (blocks,), jnp.float32, low / len(cuts), largest / len(cuts))
        return jnp.repeat(jnp.exp(draws), extent[dim] // blocks).reshape((-1,) + (1,) * (len(extent) - dim - 1))

    factor_of = one(*cuts[0])
    for cut in cuts[1:]:
        factor_of = factor_of * one(*cut)
    return factor_of


def bell_draw_with(rng, extent, width, limit, cuts, heavy, kind=jnp.bfloat16):
    values = width * jax.random.normal(rng, extent, jnp.float32)
    if cuts:
        values = values * block_levels(rng, extent, cuts, -0.22, 0.18)
    return jnp.clip(raised(values, jax.random.fold_in(rng, 3), *heavy), -limit, limit).astype(kind)


def setup_inputs(seed: int = 0) -> dict:
    splits = jax.random.split(jax.random.key(seed), 6)
    return {
        "library_bits": draw_library_bits(jax.random.fold_in(splits[5], 71), 0),
        "library_count": draw_library_count(jax.random.fold_in(splits[5], 71), 0),
        "landmark_bits": draw_landmark_bits(jax.random.fold_in(splits[5], 71), 0),
        "landmark_count": draw_landmark_count(jax.random.fold_in(splits[5], 71), 0),
        "inverse_root": bell_draw_with(splits[4], (NLM, NLM), NLM ** -0.5, 0.09375, ((0, 8), (1, 4)), (0, 1, 8, 2.0)),
    }


def tversky(row_bits, row_count, col_bits, col_count):
    common = lax.dot_general(row_bits, col_bits, (((1,), (1,)), ((), ())), preferred_element_type=jnp.float32)
    scale_sum = 0.9 * row_count.astype(jnp.float32)[:, None] + 0.1 * col_count.astype(jnp.float32)[None, :]
    return (common / scale_sum).astype(jnp.bfloat16)


def reference(library_bits, library_count, landmark_bits, landmark_count, inverse_root):
    kernel = tversky(library_bits, library_count, landmark_bits, landmark_count)
    return jnp.dot(kernel, inverse_root, preferred_element_type=jnp.float32)
```

```python
import jax
import jax.numpy as jnp
from jax import lax
from jax.sharding import PartitionSpec as P

DEPTH = 4


def tversky(row_bits, row_count, col_bits, col_count):
    common = lax.dot_general(
        row_bits, col_bits, (((1,), (1,)), ((), ())), preferred_element_type=jnp.float32
    )
    scale_sum = (
        0.9 * row_count.astype(jnp.float32)[:, None] + 0.1 * col_count.astype(jnp.float32)[None, :]
    )
    return (common / scale_sum).astype(jnp.bfloat16)


def split_sum(n_lib, n_lmk, library_bits, library_count, landmark_bits, landmark_count, inverse_root):
    layer = n_lib // DEPTH
    swap = [(i, i ^ layer) for i in range(n_lib)]
    parity = (lax.axis_index("lib") // layer) % 2
    groups = [[i for i in range(n_lib) if (i // layer) % 2 == p] for p in (0, 1)]
    root = lax.all_gather(inverse_root, "lib", axis=0, tiled=True, axis_index_groups=groups)

    rows = library_bits.shape[0]
    other_bits = lax.ppermute(library_bits, "lib", swap)
    other_count = lax.ppermute(library_count, "lib", swap)
    block = tversky(
        jnp.concatenate([other_bits, library_bits]),
        jnp.concatenate([other_count, library_count]),
        landmark_bits,
        landmark_count,
    )
    kernel = lax.all_gather(block, "lmk", axis=1, tiled=True)
    quarter = kernel.shape[1] // DEPTH
    half = jnp.concatenate(
        [lax.dynamic_slice_in_dim(kernel, (2 * k + parity) * quarter, quarter, 1) for k in (0, 1)], 1
    )
    theirs = jnp.dot(half[:rows], root, preferred_element_type=jnp.float32).astype(jnp.bfloat16)
    arrived = lax.ppermute(theirs, "lib", swap)
    mine = jnp.dot(half[rows:], root, preferred_element_type=jnp.float32)
    return mine + arrived.astype(jnp.float32)


def solution(mesh):
    placed = (P("lib", None), P("lib"), P("lmk", None), P("lmk"), P("lib", "lmk"))
    n_lib, n_lmk = mesh.shape["lib"], mesh.shape["lmk"]

    def shards(*blocks):
        return split_sum(n_lib, n_lmk, *blocks)

    return jax.shard_map(
        shards, mesh=mesh, in_specs=placed, out_specs=P("lib", "lmk"), check_vma=False
    )
```

```python
import jax
import jax.numpy as jnp
from jax import lax
from jax.experimental import pallas as pl
from jax.experimental.pallas import tpu as pltpu
from jax.sharding import PartitionSpec as P

MESH = pl.DeviceIdType.MESH
CHUNKS = 8
EARLY = 3

DEPTH = 4


def tversky(row_bits, row_count, col_bits, col_count):
    common = lax.dot_general(
        row_bits, col_bits, (((1,), (1,)), ((), ())), preferred_element_type=jnp.float32
    )
    scale_sum = (
        0.9 * row_count.astype(jnp.float32)[:, None] + 0.1 * col_count.astype(jnp.float32)[None, :]
    )
    return (common / scale_sum).astype(jnp.bfloat16)


def split_sum(n_lib, n_lmk, library_bits, library_count, landmark_bits, landmark_count, inverse_root):
    layer = n_lib // DEPTH
    swap = [(i, i ^ layer) for i in range(n_lib)]
    parity = (lax.axis_index("lib") // layer) % 2
    groups = [[i for i in range(n_lib) if (i // layer) % 2 == p] for p in (0, 1)]
    root = lax.all_gather(inverse_root, "lib", axis=0, tiled=True, axis_index_groups=groups)

    rows = library_bits.shape[0]
    other_bits = lax.ppermute(library_bits, "lib", swap)
    other_count = lax.ppermute(library_count, "lib", swap)
    block = tversky(
        jnp.concatenate([other_bits, library_bits]),
        jnp.concatenate([other_count, library_count]),
        landmark_bits,
        landmark_count,
    )
    kernel = lax.all_gather(block, "lmk", axis=1, tiled=True)
    quarter = kernel.shape[1] // DEPTH
    half = jnp.concatenate(
        [lax.dynamic_slice_in_dim(kernel, (2 * k + parity) * quarter, quarter, 1) for k in (0, 1)], 1
    )
    theirs = jnp.dot(half[:rows], root, preferred_element_type=jnp.float32).astype(jnp.bfloat16)
    arrived = lax.ppermute(theirs, "lib", swap)
    mine = jnp.dot(half[rows:], root, preferred_element_type=jnp.float32)
    return mine + arrived.astype(jnp.float32)


def body(lib_hbm, lmk_hbm, lmk_count, root_hbm, out, lib, lmk, kern, root, sent, came, load_sem,
         bits_sem, root_send, root_recv, kern_x, kern_c, kern_recv, half_send, half_recv):
    i, m = lax.axis_index("lib"), lax.axis_index("lmk")
    zh, zl, y = lax.div(i, 4), lax.rem(lax.div(i, 2), 2), lax.rem(i, 2)
    x, core = lax.div(m, 2), lax.rem(m, 2)
    by_y = (i + 1 - 2 * y, m)
    by_zl = (i + 2 - 4 * zl, m)
    by_zh = (i + 4 - 8 * zh, m)
    by_x = (i, m + 2 - 4 * x)
    by_core = (i, m + 1 - 2 * core)
    home = core == zl
    away = core != zl
    rows = lib.shape[1]
    width = root.shape[3] // CHUNKS

    def columns(j):
        return pl.ds(pl.multiple_of(j * width, width), width)

    def remote(src, dst, send, recv, peer):
        return pltpu.make_async_remote_copy(
            src_ref=src, dst_ref=dst, send_sem=send, recv_sem=recv, device_id=peer, device_id_type=MESH
        )

    def root_copy(way, j, p, q, peer, src=None):
        dst = root.at[p, q, :, columns(j)]
        src = dst if src is None else src.at[:, columns(j)]
        return remote(src, dst, root_send.at[way, j], root_recv.at[way, j], peer)

    def to_y(j):
        return root_copy(0, j, zh, y, by_y, root_hbm)

    def to_zh(j):
        return root_copy(1, j, zh, y, by_zh, root_hbm)

    def hand_on(j):
        return root_copy(2, j, 1 - zh, y, by_y)

    def bits_copy():
        return remote(lib_hbm, lib.at[1], bits_sem.at[0], bits_sem.at[1], by_zl)

    def kern_to_x(r):
        return remote(kern.at[x, r], kern.at[x, r], kern_x.at[r], kern_recv.at[x, r], by_x)

    def kern_from_x(r):
        return remote(kern.at[1 - x, r], kern.at[1 - x, r], kern_x.at[r], kern_recv.at[1 - x, r], by_x)

    def kern_to_core(p, r):
        return remote(kern.at[p, r], kern.at[p, r], kern_c.at[p, r], kern_recv.at[p, r], by_core)

    def half_copy(j):
        return remote(
            sent.at[:, columns(j)], came.at[:, columns(j)], half_send.at[j], half_recv.at[j], by_zl
        )

    barrier = pltpu.get_barrier_semaphore()
    for peer in (by_y, by_zl, by_zh, by_x, by_core):
        pl.semaphore_signal(barrier, inc=1, device_id=peer, device_id_type=MESH)
    pl.semaphore_wait(barrier, 5)

    @pl.when(away)
    def _():
        bits_copy().start()

    @pl.loop(0, CHUNKS)
    def _(j):
        to_zh(j).start()
        to_y(j).start()

    load_root = pltpu.make_async_copy(root_hbm, root.at[zh, y], load_sem.at[0])
    load_lib = pltpu.make_async_copy(lib_hbm, lib.at[0], load_sem.at[1])
    load_lmk = pltpu.make_async_copy(lmk_hbm, lmk, load_sem.at[2])

    def tversky_rows(r):
        ones = jnp.ones((lib.shape[2], 128), jnp.bfloat16)
        row_count = jnp.dot(lib[r], ones, preferred_element_type=jnp.float32)[:, :1]
        step = min(256, lmk.shape[0])

        @pl.loop(0, lmk.shape[0] // step)
        def _(k):
            at = pl.ds(pl.multiple_of(k * step, step), step)
            common = lax.dot_general(
                lib[r], lmk[at, :], (((1,), (1,)), ((), ())), preferred_element_type=jnp.float32
            )
            scale_sum = 0.9 * row_count + 0.1 * lmk_count[:, at].astype(jnp.float32)
            kern[x, r, :, at] = (common / scale_sum).astype(jnp.bfloat16)

        kern_to_x(r).start()
        kern_to_core(x, r).start()

    @pl.when(home)
    def _():
        load_lib.start()
        load_lmk.start()
        load_root.start()
        load_lib.wait()
        load_lmk.wait()
        tversky_rows(0)
        bits_copy().wait_recv()
        tversky_rows(1)

    @pl.when(away)
    def _():
        load_root.start()

    @pl.loop(0, EARLY)
    def _(j):
        to_zh(j).wait_recv()
        hand_on(j).start()

    @pl.when(home)
    def _():
        @pl.loop(0, 2)
        def _(r):
            kern_from_x(r).wait_recv()
            kern_to_core(1 - x, r).start()

    @pl.when(away)
    def _():
        @pl.loop(0, 2)
        def _(r):
            kern_to_core(x, r).wait_recv()
            kern_to_core(1 - x, r).wait_recv()

    load_root.wait()

    def finish(j):
        half_copy(j).wait_recv()
        out[:, columns(j)] += came[:, columns(j)].astype(jnp.float32)

    def half_sum(r, j):
        depth = 2 * root.shape[2]
        return sum(
            jnp.dot(
                kern[p, r],
                root[p, :, :, columns(j)].reshape(depth, width),
                preferred_element_type=jnp.float32,
            )
            for p in (0, 1)
        )

    @pl.loop(0, CHUNKS)
    def _(j):
        @pl.when(j >= EARLY)
        def _():
            to_zh(j).wait_recv()
            hand_on(j).start()

        to_y(j).wait_recv()
        hand_on(j).wait_recv()
        sent[:, columns(j)] = half_sum(1, j).astype(jnp.bfloat16)
        half_copy(j).start()
        out[:, columns(j)] = half_sum(0, j)

        @pl.when(j > 0)
        def _():
            finish(j - 1)

    finish(CHUNKS - 1)

    @pl.loop(0, CHUNKS)
    def _(j):
        to_y(j).wait_send()
        to_zh(j).wait_send()
        hand_on(j).wait_send()
        half_copy(j).wait_send()

    @pl.when(away)
    def _():
        bits_copy().wait_send()

    @pl.when(home)
    def _():
        @pl.loop(0, 2)
        def _(r):
            kern_to_x(r).wait_send()
            kern_to_core(x, r).wait_send()
            kern_to_core(1 - x, r).wait_send()


def one_kernel(library_bits, library_count, landmark_bits, landmark_count, inverse_root):
    del library_count
    rows, bits = library_bits.shape
    lmks = landmark_bits.shape[0]
    depth, cols = inverse_root.shape
    hbm = pl.BlockSpec(memory_space=pl.ANY)
    vmem = pl.BlockSpec(memory_space=pltpu.VMEM)
    dma = pltpu.SemaphoreType.DMA
    return pl.pallas_call(
        body,
        out_shape=jax.ShapeDtypeStruct((rows, cols), jnp.float32),
        in_specs=[hbm, hbm, vmem, hbm],
        out_specs=vmem,
        scratch_shapes=[
            pltpu.VMEM((2, rows, bits), jnp.bfloat16),
            pltpu.VMEM((lmks, bits), jnp.bfloat16),
            pltpu.VMEM((2, 2, rows, lmks), jnp.bfloat16),
            pltpu.VMEM((2, 2, depth, cols), jnp.bfloat16),
            pltpu.VMEM((rows, cols), jnp.bfloat16),
            pltpu.VMEM((rows, cols), jnp.bfloat16),
            dma((3,)),
            dma((2,)),
            dma((3, CHUNKS)),
            dma((3, CHUNKS)),
            dma((2,)),
            dma((2, 2)),
            dma((2, 2)),
            dma((CHUNKS,)),
            dma((CHUNKS,)),
        ],
        compiler_params=pltpu.CompilerParams(
            collective_id=0, has_side_effects=True, vmem_limit_bytes=60 * 1024 * 1024
        ),
        cost_estimate=pl.CostEstimate(
            flops=2 * rows * (lmks * bits + 4 * lmks * cols),
            bytes_accessed=2 * (rows * bits + lmks * bits + depth * cols) + 4 * rows * cols,
            transcendentals=0,
        ),
    )(library_bits, landmark_bits, landmark_count.reshape(1, lmks), inverse_root)


def solution(mesh):
    placed = (P("lib", None), P("lib"), P("lmk", None), P("lmk"), P("lib", "lmk"))
    n_lib, n_lmk = mesh.shape["lib"], mesh.shape["lmk"]

    def shards(*blocks):
        if (n_lib, n_lmk) == (8, 4):
            return one_kernel(*blocks)
        return split_sum(n_lib, n_lmk, *blocks)

    return jax.shard_map(
        shards, mesh=mesh, in_specs=placed, out_specs=P("lib", "lmk"), check_vma=False
    )
```

```python
import jax
import jax.numpy as jnp
from jax import lax
from jax.experimental import pallas as pl
from jax.experimental.pallas import tpu as pltpu
from jax.sharding import PartitionSpec as P

MESH = pl.DeviceIdType.MESH
CHUNKS = 8
AHEAD = 2
EARLY = 3

DEPTH = 4


def tversky(row_bits, row_count, col_bits, col_count):
    common = lax.dot_general(
        row_bits, col_bits, (((1,), (1,)), ((), ())), preferred_element_type=jnp.float32
    )
    scale_sum = (
        0.9 * row_count.astype(jnp.float32)[:, None] + 0.1 * col_count.astype(jnp.float32)[None, :]
    )
    return (common / scale_sum).astype(jnp.bfloat16)


def split_sum(n_lib, n_lmk, library_bits, library_count, landmark_bits, landmark_count, inverse_root):
    layer = n_lib // DEPTH
    swap = [(i, i ^ layer) for i in range(n_lib)]
    parity = (lax.axis_index("lib") // layer) % 2
    groups = [[i for i in range(n_lib) if (i // layer) % 2 == p] for p in (0, 1)]
    root = lax.all_gather(inverse_root, "lib", axis=0, tiled=True, axis_index_groups=groups)

    rows = library_bits.shape[0]
    other_bits = lax.ppermute(library_bits, "lib", swap)
    other_count = lax.ppermute(library_count, "lib", swap)
    block = tversky(
        jnp.concatenate([other_bits, library_bits]),
        jnp.concatenate([other_count, library_count]),
        landmark_bits,
        landmark_count,
    )
    kernel = lax.all_gather(block, "lmk", axis=1, tiled=True)
    quarter = kernel.shape[1] // DEPTH
    half = jnp.concatenate(
        [lax.dynamic_slice_in_dim(kernel, (2 * k + parity) * quarter, quarter, 1) for k in (0, 1)], 1
    )
    theirs = jnp.dot(half[:rows], root, preferred_element_type=jnp.float32).astype(jnp.bfloat16)
    arrived = lax.ppermute(theirs, "lib", swap)
    mine = jnp.dot(half[rows:], root, preferred_element_type=jnp.float32)
    return mine + arrived.astype(jnp.float32)


def body(lib_hbm, lmk_hbm, lmk_count, root_hbm, out, lib, lmk, kern, root, sent, came, load_sem,
         bits_sem, root_send, root_recv, kern_x, kern_c, kern_recv, half_send, half_recv):
    i, m = lax.axis_index("lib"), lax.axis_index("lmk")
    zh, zl, y = lax.div(i, 4), lax.rem(lax.div(i, 2), 2), lax.rem(i, 2)
    x, core = lax.div(m, 2), lax.rem(m, 2)
    by_y = (i + 1 - 2 * y, m)
    by_zl = (i + 2 - 4 * zl, m)
    by_zh = (i + 4 - 8 * zh, m)
    by_x = (i, m + 2 - 4 * x)
    by_core = (i, m + 1 - 2 * core)
    home = core == zl
    away = core != zl
    rows = lib.shape[1]
    width = root.shape[3] // CHUNKS

    def columns(j):
        return pl.ds(pl.multiple_of(j * width, width), width)

    def remote(src, dst, send, recv, peer):
        return pltpu.make_async_remote_copy(
            src_ref=src, dst_ref=dst, send_sem=send, recv_sem=recv, device_id=peer, device_id_type=MESH
        )

    def root_copy(way, j, p, q, peer, src=None):
        dst = root.at[p, q, :, columns(j)]
        src = dst if src is None else src.at[:, columns(j)]
        return remote(src, dst, root_send.at[way, j], root_recv.at[way, j], peer)

    def to_y(j):
        return root_copy(0, j, zh, y, by_y, root_hbm)

    def to_zh(j):
        return root_copy(1, j, zh, y, by_zh, root_hbm)

    def hand_on(j):
        return root_copy(2, j, 1 - zh, y, by_y)

    def bits_copy():
        return remote(lib_hbm, lib.at[1], bits_sem.at[0], bits_sem.at[1], by_zl)

    def kern_to_x(r):
        return remote(kern.at[x, r], kern.at[x, r], kern_x.at[r], kern_recv.at[x, r], by_x)

    def kern_from_x(r):
        return remote(kern.at[1 - x, r], kern.at[1 - x, r], kern_x.at[r], kern_recv.at[1 - x, r], by_x)

    def kern_to_core(p, r):
        return remote(kern.at[p, r], kern.at[p, r], kern_c.at[p, r], kern_recv.at[p, r], by_core)

    def half_copy(j):
        return remote(
            sent.at[:, columns(j)], came.at[:, columns(j)], half_send.at[j], half_recv.at[j], by_zl
        )

    barrier = pltpu.get_barrier_semaphore()
    for peer in (by_y, by_zl, by_zh, by_x, by_core):
        pl.semaphore_signal(barrier, inc=1, device_id=peer, device_id_type=MESH)
    pl.semaphore_wait(barrier, 5)

    @pl.when(away)
    def _():
        bits_copy().start()

    @pl.loop(0, AHEAD)
    def _(j):
        to_zh(j).start()
        to_y(j).start()

    def serve(j):
        to_zh(j).wait_recv()
        hand_on(j).start()

        @pl.when(j + AHEAD < CHUNKS)
        def _():
            to_zh(j).wait_send()
            to_zh(j + AHEAD).start()
            to_y(j).wait_send()
            to_y(j + AHEAD).start()

    load_root = pltpu.make_async_copy(root_hbm, root.at[zh, y], load_sem.at[0])
    load_lib = pltpu.make_async_copy(lib_hbm, lib.at[0], load_sem.at[1])
    load_lmk = pltpu.make_async_copy(lmk_hbm, lmk, load_sem.at[2])

    def tversky_rows(r):
        ones = jnp.ones((lib.shape[2], 128), jnp.bfloat16)
        row_count = jnp.dot(lib[r], ones, preferred_element_type=jnp.float32)[:, :1]
        step = min(256, lmk.shape[0])

        @pl.loop(0, lmk.shape[0] // step)
        def _(k):
            at = pl.ds(pl.multiple_of(k * step, step), step)
            common = lax.dot_general(
                lib[r], lmk[at, :], (((1,), (1,)), ((), ())), preferred_element_type=jnp.float32
            )
            scale_sum = 0.9 * row_count + 0.1 * lmk_count[:, at].astype(jnp.float32)
            kern[x, r, :, at] = (common / scale_sum).astype(jnp.bfloat16)

        kern_to_x(r).start()
        kern_to_core(x, r).start()

    @pl.when(home)
    def _():
        load_lib.start()
        load_lmk.start()
        load_root.start()
        load_lib.wait()
        load_lmk.wait()
        tversky_rows(0)

    @pl.when(away)
    def _():
        load_root.start()

    @pl.loop(0, EARLY)
    def _(j):
        serve(j)

        @pl.when(home & (j == 0))
        def _():
            bits_copy().wait_recv()
            tversky_rows(1)

        @pl.when(home & (j > 0))
        def _():
            kern_from_x(j - 1).wait_recv()
            kern_to_core(1 - x, j - 1).start()

    @pl.when(away)
    def _():
        @pl.loop(0, 2)
        def _(r):
            kern_to_core(x, r).wait_recv()
            kern_to_core(1 - x, r).wait_recv()

    load_root.wait()

    def finish(j):
        half_copy(j).wait_recv()
        out[:, columns(j)] += came[:, columns(j)].astype(jnp.float32)

    def half_sum(r, j):
        depth = 2 * root.shape[2]
        return sum(
            jnp.dot(
                kern[p, r],
                root[p, :, :, columns(j)].reshape(depth, width),
                preferred_element_type=jnp.float32,
            )
            for p in (0, 1)
        )

    @pl.loop(0, CHUNKS)
    def _(j):
        @pl.when(j >= EARLY)
        def _():
            serve(j)

        to_y(j).wait_recv()
        hand_on(j).wait_recv()
        sent[:, columns(j)] = half_sum(1, j).astype(jnp.bfloat16)
        half_copy(j).start()
        out[:, columns(j)] = half_sum(0, j)

        @pl.when(j > 0)
        def _():
            finish(j - 1)

    finish(CHUNKS - 1)

    @pl.loop(CHUNKS - AHEAD, CHUNKS)
    def _(j):
        to_y(j).wait_send()
        to_zh(j).wait_send()

    @pl.loop(0, CHUNKS)
    def _(j):
        hand_on(j).wait_send()
        half_copy(j).wait_send()

    @pl.when(away)
    def _():
        bits_copy().wait_send()

    @pl.when(home)
    def _():
        @pl.loop(0, 2)
        def _(r):
            kern_to_x(r).wait_send()
            kern_to_core(x, r).wait_send()
            kern_to_core(1 - x, r).wait_send()


def one_kernel(library_bits, library_count, landmark_bits, landmark_count, inverse_root):
    del library_count
    rows, bits = library_bits.shape
    lmks = landmark_bits.shape[0]
    depth, cols = inverse_root.shape
    hbm = pl.BlockSpec(memory_space=pl.ANY)
    vmem = pl.BlockSpec(memory_space=pltpu.VMEM)
    dma = pltpu.SemaphoreType.DMA
    return pl.pallas_call(
        body,
        out_shape=jax.ShapeDtypeStruct((rows, cols), jnp.float32),
        in_specs=[hbm, hbm, vmem, hbm],
        out_specs=vmem,
        scratch_shapes=[
            pltpu.VMEM((2, rows, bits), jnp.bfloat16),
            pltpu.VMEM((lmks, bits), jnp.bfloat16),
            pltpu.VMEM((2, 2, rows, lmks), jnp.bfloat16),
            pltpu.VMEM((2, 2, depth, cols), jnp.bfloat16),
            pltpu.VMEM((rows, cols), jnp.bfloat16),
            pltpu.VMEM((rows, cols), jnp.bfloat16),
            dma((3,)),
            dma((2,)),
            dma((3, CHUNKS)),
            dma((3, CHUNKS)),
            dma((2,)),
            dma((2, 2)),
            dma((2, 2)),
            dma((CHUNKS,)),
            dma((CHUNKS,)),
        ],
        compiler_params=pltpu.CompilerParams(
            collective_id=0, has_side_effects=True, vmem_limit_bytes=60 * 1024 * 1024
        ),
        cost_estimate=pl.CostEstimate(
            flops=2 * rows * (lmks * bits + 4 * lmks * cols),
            bytes_accessed=2 * (rows * bits + lmks * bits + depth * cols) + 4 * rows * cols,
            transcendentals=0,
        ),
    )(library_bits, landmark_bits, landmark_count.reshape(1, lmks), inverse_root)


def solution(mesh):
    placed = (P("lib", None), P("lib"), P("lmk", None), P("lmk"), P("lib", "lmk"))
    n_lib, n_lmk = mesh.shape["lib"], mesh.shape["lmk"]

    def shards(*blocks):
        if (n_lib, n_lmk) == (8, 4):
            return one_kernel(*blocks)
        return split_sum(n_lib, n_lmk, *blocks)

    return jax.shard_map(
        shards, mesh=mesh, in_specs=placed, out_specs=P("lib", "lmk"), check_vma=False
    )
```

```python
import jax
import jax.numpy as jnp
from jax import lax
from jax.experimental import pallas as pl
from jax.experimental.pallas import tpu as pltpu
from jax.sharding import PartitionSpec as P

MESH = pl.DeviceIdType.MESH
CHUNKS = 16
AHEAD = 4
EARLY = 6
PIECES = 3

DEPTH = 4


def tversky(row_bits, row_count, col_bits, col_count):
    common = lax.dot_general(
        row_bits, col_bits, (((1,), (1,)), ((), ())), preferred_element_type=jnp.float32
    )
    scale_sum = (
        0.9 * row_count.astype(jnp.float32)[:, None] + 0.1 * col_count.astype(jnp.float32)[None, :]
    )
    return (common / scale_sum).astype(jnp.bfloat16)


def split_sum(n_lib, n_lmk, library_bits, library_count, landmark_bits, landmark_count, inverse_root):
    layer = n_lib // DEPTH
    swap = [(i, i ^ layer) for i in range(n_lib)]
    parity = (lax.axis_index("lib") // layer) % 2
    groups = [[i for i in range(n_lib) if (i // layer) % 2 == p] for p in (0, 1)]
    root = lax.all_gather(inverse_root, "lib", axis=0, tiled=True, axis_index_groups=groups)

    rows = library_bits.shape[0]
    other_bits = lax.ppermute(library_bits, "lib", swap)
    other_count = lax.ppermute(library_count, "lib", swap)
    block = tversky(
        jnp.concatenate([other_bits, library_bits]),
        jnp.concatenate([other_count, library_count]),
        landmark_bits,
        landmark_count,
    )
    kernel = lax.all_gather(block, "lmk", axis=1, tiled=True)
    quarter = kernel.shape[1] // DEPTH
    half = jnp.concatenate(
        [lax.dynamic_slice_in_dim(kernel, (2 * k + parity) * quarter, quarter, 1) for k in (0, 1)], 1
    )
    theirs = jnp.dot(half[:rows], root, preferred_element_type=jnp.float32).astype(jnp.bfloat16)
    arrived = lax.ppermute(theirs, "lib", swap)
    mine = jnp.dot(half[rows:], root, preferred_element_type=jnp.float32)
    return mine + arrived.astype(jnp.float32)


def body(lib_hbm, lmk_hbm, lmk_count, root_hbm, out, lib, lmk, kern, root, sent, came, load_sem,
         bits_sem, root_send, root_recv, kern_x, kern_c, kern_recv, half_send, half_recv):
    i, m = lax.axis_index("lib"), lax.axis_index("lmk")
    zh, zl, y = lax.div(i, 4), lax.rem(lax.div(i, 2), 2), lax.rem(i, 2)
    x, core = lax.div(m, 2), lax.rem(m, 2)
    by_y = (i + 1 - 2 * y, m)
    by_zl = (i + 2 - 4 * zl, m)
    by_zh = (i + 4 - 8 * zh, m)
    by_x = (i, m + 2 - 4 * x)
    by_core = (i, m + 1 - 2 * core)
    home = core == zl
    away = core != zl
    rows = lib.shape[1]
    part = rows // PIECES
    width = root.shape[3] // CHUNKS

    def columns(j):
        return pl.ds(pl.multiple_of(j * width, width), width)

    def remote(src, dst, send, recv, peer):
        return pltpu.make_async_remote_copy(
            src_ref=src, dst_ref=dst, send_sem=send, recv_sem=recv, device_id=peer, device_id_type=MESH
        )

    def root_copy(way, j, p, q, peer, src=None):
        dst = root.at[p, q, :, columns(j)]
        src = dst if src is None else src.at[:, columns(j)]
        return remote(src, dst, root_send.at[way, j], root_recv.at[way, j], peer)

    def to_y(j):
        return root_copy(0, j, zh, y, by_y, root_hbm)

    def to_zh(j):
        return root_copy(1, j, zh, y, by_zh, root_hbm)

    def hand_on(j):
        return root_copy(2, j, 1 - zh, y, by_y)

    def piece(q):
        return pl.ds(pl.multiple_of(q * part, part), part)

    def bits_copy(q):
        return remote(
            lib_hbm.at[piece(q)], lib.at[1, piece(q)], bits_sem.at[0, q], bits_sem.at[1, q], by_zl
        )

    def kern_copy(p, r, q, send, peer):
        at = kern.at[p, r, piece(q)]
        return remote(at, at, send, kern_recv.at[p, r, q], peer)

    def kern_to_x(r, q):
        return kern_copy(x, r, q, kern_x.at[r, q], by_x)

    def kern_from_x(r, q):
        return kern_copy(1 - x, r, q, kern_x.at[r, q], by_x)

    def kern_to_core(p, r, q):
        return kern_copy(p, r, q, kern_c.at[p, r, q], by_core)

    def each_piece(step):
        pl.loop(0, PIECES)(step)

    def half_copy(j):
        return remote(
            sent.at[:, columns(j)], came.at[:, columns(j)], half_send.at[j], half_recv.at[j], by_zl
        )

    barrier = pltpu.get_barrier_semaphore()
    for peer in (by_y, by_zl, by_zh, by_x, by_core):
        pl.semaphore_signal(barrier, inc=1, device_id=peer, device_id_type=MESH)
    pl.semaphore_wait(barrier, 5)

    @pl.when(away)
    def _():
        each_piece(lambda q: bits_copy(q).start())

    @pl.loop(0, AHEAD)
    def _(j):
        to_zh(j).start()
        to_y(j).start()

    def serve(j):
        to_zh(j).wait_recv()
        hand_on(j).start()

        @pl.when(j + AHEAD < CHUNKS)
        def _():
            to_zh(j).wait_send()
            to_zh(j + AHEAD).start()
            to_y(j).wait_send()
            to_y(j + AHEAD).start()

    load_root = pltpu.make_async_copy(root_hbm, root.at[zh, y], load_sem.at[0])
    load_lib = pltpu.make_async_copy(lib_hbm, lib.at[0], load_sem.at[1])
    load_lmk = pltpu.make_async_copy(lmk_hbm, lmk, load_sem.at[2])

    def tversky_piece(r, q):
        ones = jnp.ones((lib.shape[2], 128), jnp.bfloat16)
        row_count = jnp.dot(lib[r, piece(q)], ones, preferred_element_type=jnp.float32)[:, :1]
        step = min(256, lmk.shape[0])

        @pl.loop(0, lmk.shape[0] // step)
        def _(k):
            at = pl.ds(pl.multiple_of(k * step, step), step)
            common = lax.dot_general(
                lib[r, piece(q)],
                lmk[at, :],
                (((1,), (1,)), ((), ())),
                preferred_element_type=jnp.float32,
            )
            scale_sum = 0.9 * row_count + 0.1 * lmk_count[:, at].astype(jnp.float32)
            kern[x, r, piece(q), at] = (common / scale_sum).astype(jnp.bfloat16)

        kern_to_x(r, q).start()
        kern_to_core(x, r, q).start()

    def pass_to_core(r, q):
        kern_from_x(r, q).wait_recv()
        kern_to_core(1 - x, r, q).start()

    @pl.when(home)
    def _():
        load_lib.start()
        load_lmk.start()
        load_root.start()
        load_lib.wait()
        load_lmk.wait()
        each_piece(lambda q: tversky_piece(0, q))

    @pl.when(away)
    def _():
        load_root.start()

    @pl.loop(0, EARLY)
    def _(j):
        serve(j)

        @pl.when(home & (lax.rem(j, 2) == 1))
        def _():
            q = lax.div(j, 2)
            bits_copy(q).wait_recv()
            tversky_piece(1, q)

        @pl.when(home & (j == 4))
        def _():
            each_piece(lambda q: pass_to_core(0, q))

    @pl.when(home)
    def _():
        each_piece(lambda q: pass_to_core(1, q))

    @pl.when(away)
    def _():
        @pl.loop(0, 2)
        def _(r):
            each_piece(lambda q: kern_to_core(x, r, q).wait_recv())
            each_piece(lambda q: kern_to_core(1 - x, r, q).wait_recv())

    load_root.wait()

    def finish(j):
        half_copy(j).wait_recv()
        out[:, columns(j)] += came[:, columns(j)].astype(jnp.float32)

    def half_sum(r, j):
        depth = 2 * root.shape[2]
        return sum(
            jnp.dot(
                kern[p, r],
                root[p, :, :, columns(j)].reshape(depth, width),
                preferred_element_type=jnp.float32,
            )
            for p in (0, 1)
        )

    @pl.loop(0, CHUNKS)
    def _(j):
        @pl.when(j >= EARLY)
        def _():
            serve(j)

        to_y(j).wait_recv()
        hand_on(j).wait_recv()
        sent[:, columns(j)] = half_sum(1, j).astype(jnp.bfloat16)
        half_copy(j).start()
        out[:, columns(j)] = half_sum(0, j)

        @pl.when(j > 0)
        def _():
            finish(j - 1)

    finish(CHUNKS - 1)

    @pl.loop(CHUNKS - AHEAD, CHUNKS)
    def _(j):
        to_y(j).wait_send()
        to_zh(j).wait_send()

    @pl.loop(0, CHUNKS)
    def _(j):
        hand_on(j).wait_send()
        half_copy(j).wait_send()

    @pl.when(away)
    def _():
        each_piece(lambda q: bits_copy(q).wait_send())

    @pl.when(home)
    def _():
        @pl.loop(0, 2)
        def _(r):
            each_piece(lambda q: kern_to_x(r, q).wait_send())
            each_piece(lambda q: kern_to_core(x, r, q).wait_send())
            each_piece(lambda q: kern_to_core(1 - x, r, q).wait_send())


def one_kernel(library_bits, library_count, landmark_bits, landmark_count, inverse_root):
    del library_count
    rows, bits = library_bits.shape
    lmks = landmark_bits.shape[0]
    depth, cols = inverse_root.shape
    hbm = pl.BlockSpec(memory_space=pl.ANY)
    vmem = pl.BlockSpec(memory_space=pltpu.VMEM)
    dma = pltpu.SemaphoreType.DMA
    return pl.pallas_call(
        body,
        out_shape=jax.ShapeDtypeStruct((rows, cols), jnp.float32),
        in_specs=[hbm, hbm, vmem, hbm],
        out_specs=vmem,
        scratch_shapes=[
            pltpu.VMEM((2, rows, bits), jnp.bfloat16),
            pltpu.VMEM((lmks, bits), jnp.bfloat16),
            pltpu.VMEM((2, 2, rows, lmks), jnp.bfloat16),
            pltpu.VMEM((2, 2, depth, cols), jnp.bfloat16),
            pltpu.VMEM((rows, cols), jnp.bfloat16),
            pltpu.VMEM((rows, cols), jnp.bfloat16),
            dma((3,)),
            dma((2, PIECES)),
            dma((3, CHUNKS)),
            dma((3, CHUNKS)),
            dma((2, PIECES)),
            dma((2, 2, PIECES)),
            dma((2, 2, PIECES)),
            dma((CHUNKS,)),
            dma((CHUNKS,)),
        ],
        compiler_params=pltpu.CompilerParams(
            collective_id=0, has_side_effects=True, vmem_limit_bytes=60 * 1024 * 1024
        ),
        cost_estimate=pl.CostEstimate(
            flops=2 * rows * (lmks * bits + 4 * lmks * cols),
            bytes_accessed=2 * (rows * bits + lmks * bits + depth * cols) + 4 * rows * cols,
            transcendentals=0,
        ),
    )(library_bits, landmark_bits, landmark_count.reshape(1, lmks), inverse_root)


def solution(mesh):
    placed = (P("lib", None), P("lib"), P("lmk", None), P("lmk"), P("lib", "lmk"))
    n_lib, n_lmk = mesh.shape["lib"], mesh.shape["lmk"]

    def shards(*blocks):
        if (n_lib, n_lmk) == (8, 4):
            return one_kernel(*blocks)
        return split_sum(n_lib, n_lmk, *blocks)

    return jax.shard_map(
        shards, mesh=mesh, in_specs=placed, out_specs=P("lib", "lmk"), check_vma=False
    )
```

```python
import jax
import jax.numpy as jnp
from jax import lax
from jax.experimental import pallas as pl
from jax.experimental.pallas import tpu as pltpu
from jax.sharding import PartitionSpec as P

MESH = pl.DeviceIdType.MESH
CHUNKS = 8
AHEAD = 2
PIECES = 3
EARLY = PIECES

DEPTH = 4


def tversky(row_bits, row_count, col_bits, col_count):
    common = lax.dot_general(
        row_bits, col_bits, (((1,), (1,)), ((), ())), preferred_element_type=jnp.float32
    )
    scale_sum = (
        0.9 * row_count.astype(jnp.float32)[:, None] + 0.1 * col_count.astype(jnp.float32)[None, :]
    )
    return (common / scale_sum).astype(jnp.bfloat16)


def split_sum(n_lib, n_lmk, library_bits, library_count, landmark_bits, landmark_count, inverse_root):
    layer = n_lib // DEPTH
    swap = [(i, i ^ layer) for i in range(n_lib)]
    parity = (lax.axis_index("lib") // layer) % 2
    groups = [[i for i in range(n_lib) if (i // layer) % 2 == p] for p in (0, 1)]
    root = lax.all_gather(inverse_root, "lib", axis=0, tiled=True, axis_index_groups=groups)

    rows = library_bits.shape[0]
    other_bits = lax.ppermute(library_bits, "lib", swap)
    other_count = lax.ppermute(library_count, "lib", swap)
    block = tversky(
        jnp.concatenate([other_bits, library_bits]),
        jnp.concatenate([other_count, library_count]),
        landmark_bits,
        landmark_count,
    )
    kernel = lax.all_gather(block, "lmk", axis=1, tiled=True)
    quarter = kernel.shape[1] // DEPTH
    half = jnp.concatenate(
        [lax.dynamic_slice_in_dim(kernel, (2 * k + parity) * quarter, quarter, 1) for k in (0, 1)], 1
    )
    theirs = jnp.dot(half[:rows], root, preferred_element_type=jnp.float32).astype(jnp.bfloat16)
    arrived = lax.ppermute(theirs, "lib", swap)
    mine = jnp.dot(half[rows:], root, preferred_element_type=jnp.float32)
    return mine + arrived.astype(jnp.float32)


def body(lib_hbm, lmk_hbm, lmk_count, root_hbm, out, lib, lmk, kern, root, sent, came, root_sem,
         load_sem, bits_sem, root_send, root_recv, kern_x, kern_c, kern_recv, half_send, half_recv):
    i, m = lax.axis_index("lib"), lax.axis_index("lmk")
    zh, zl, y = lax.div(i, 4), lax.rem(lax.div(i, 2), 2), lax.rem(i, 2)
    x, core = lax.div(m, 2), lax.rem(m, 2)
    by_y = (i + 1 - 2 * y, m)
    by_zl = (i + 2 - 4 * zl, m)
    by_zh = (i + 4 - 8 * zh, m)
    by_x = (i, m + 2 - 4 * x)
    by_core = (i, m + 1 - 2 * core)
    home = core == zl
    away = core != zl
    rows = lib.shape[1]
    part = rows // PIECES
    width = root.shape[4]

    def columns(j):
        return pl.ds(pl.multiple_of(j * width, width), width)

    def remote(src, dst, send, recv, peer):
        return pltpu.make_async_remote_copy(
            src_ref=src, dst_ref=dst, send_sem=send, recv_sem=recv, device_id=peer, device_id_type=MESH
        )

    def load_root(j):
        return pltpu.make_async_copy(root_hbm.at[:, columns(j)], root.at[zh, y, j], root_sem.at[j])

    def root_copy(way, j, p, q, peer):
        at = root.at[p, q, j]
        return remote(at, at, root_send.at[way, j], root_recv.at[way, j], peer)

    def to_y(j):
        return root_copy(0, j, zh, y, by_y)

    def to_zh(j):
        return root_copy(1, j, zh, y, by_zh)

    def hand_on(j):
        return root_copy(2, j, 1 - zh, y, by_y)

    def piece(q):
        return pl.ds(pl.multiple_of(q * part, part), part)

    def bits_copy(q):
        return remote(
            lib_hbm.at[piece(q)], lib.at[1, piece(q)], bits_sem.at[0, q], bits_sem.at[1, q], by_zl
        )

    def kern_copy(p, r, q, send, peer):
        at = kern.at[p, r, piece(q)]
        return remote(at, at, send, kern_recv.at[p, r, q], peer)

    def kern_to_x(r, q):
        return kern_copy(x, r, q, kern_x.at[r, q], by_x)

    def kern_from_x(r, q):
        return kern_copy(1 - x, r, q, kern_x.at[r, q], by_x)

    def kern_to_core(p, r, q):
        return kern_copy(p, r, q, kern_c.at[p, r, q], by_core)

    def each_piece(step):
        pl.loop(0, PIECES)(step)

    def half_copy(j):
        return remote(
            sent.at[j], came.at[j], half_send.at[j], half_recv.at[j], by_zl
        )

    load_lib = pltpu.make_async_copy(lib_hbm, lib.at[0], load_sem.at[0])
    load_lmk = pltpu.make_async_copy(lmk_hbm, lmk, load_sem.at[1])

    @pl.loop(0, CHUNKS)
    def _(j):
        load_root(j).start()

    @pl.when(home)
    def _():
        load_lib.start()
        load_lmk.start()

    barrier = pltpu.get_barrier_semaphore()
    for peer in (by_y, by_zl, by_zh, by_x, by_core):
        pl.semaphore_signal(barrier, inc=1, device_id=peer, device_id_type=MESH)
    pl.semaphore_wait(barrier, 5)

    @pl.when(away)
    def _():
        each_piece(lambda q: bits_copy(q).start())

    @pl.loop(0, AHEAD)
    def _(j):
        load_root(j).wait()
        to_zh(j).start()
        to_y(j).start()

    @pl.loop(AHEAD, CHUNKS)
    def _(j):
        load_root(j).wait()

    def serve(j):
        to_zh(j).wait_recv()
        hand_on(j).start()

        @pl.when(j + AHEAD < CHUNKS)
        def _():
            to_zh(j).wait_send()
            to_zh(j + AHEAD).start()
            to_y(j).wait_send()
            to_y(j + AHEAD).start()

    def tversky_piece(r, q):
        ones = jnp.ones((lib.shape[2], 128), jnp.bfloat16)
        row_count = jnp.dot(lib[r, piece(q)], ones, preferred_element_type=jnp.float32)[:, :1]
        step = min(256, lmk.shape[0])

        @pl.loop(0, lmk.shape[0] // step)
        def _(k):
            at = pl.ds(pl.multiple_of(k * step, step), step)
            common = lax.dot_general(
                lib[r, piece(q)],
                lmk[at, :],
                (((1,), (1,)), ((), ())),
                preferred_element_type=jnp.float32,
            )
            scale_sum = 0.9 * row_count + 0.1 * lmk_count[:, at].astype(jnp.float32)
            kern[x, r, piece(q), at] = (common / scale_sum).astype(jnp.bfloat16)

        kern_to_x(r, q).start()
        kern_to_core(x, r, q).start()

    def pass_to_core(r, q):
        kern_from_x(r, q).wait_recv()
        kern_to_core(1 - x, r, q).start()

    @pl.when(home)
    def _():
        load_lib.wait()
        load_lmk.wait()
        each_piece(lambda q: tversky_piece(0, q))

    @pl.loop(0, EARLY)
    def _(j):
        serve(j)

        @pl.when(home)
        def _():
            bits_copy(j).wait_recv()
            tversky_piece(1, j)

        @pl.when(home & (j == 1))
        def _():
            each_piece(lambda q: pass_to_core(0, q))

    @pl.when(home)
    def _():
        each_piece(lambda q: pass_to_core(1, q))

    @pl.when(away)
    def _():
        @pl.loop(0, 2)
        def _(r):
            each_piece(lambda q: kern_to_core(x, r, q).wait_recv())
            each_piece(lambda q: kern_to_core(1 - x, r, q).wait_recv())

    def finish(j):
        half_copy(j).wait_recv()
        out[:, columns(j)] += came[j].astype(jnp.float32)

    def half_sum(r, j):
        depth = 2 * root.shape[3]
        return sum(
            jnp.dot(
                kern[p, r],
                root[p, :, j].reshape(depth, width),
                preferred_element_type=jnp.float32,
            )
            for p in (0, 1)
        )

    @pl.loop(0, CHUNKS)
    def _(j):
        @pl.when(j >= EARLY)
        def _():
            serve(j)

        to_y(j).wait_recv()
        hand_on(j).wait_recv()
        sent[j] = half_sum(1, j).astype(jnp.bfloat16)
        half_copy(j).start()
        out[:, columns(j)] = half_sum(0, j)

        @pl.when(j > 0)
        def _():
            finish(j - 1)

    finish(CHUNKS - 1)

    @pl.loop(CHUNKS - AHEAD, CHUNKS)
    def _(j):
        to_y(j).wait_send()
        to_zh(j).wait_send()

    @pl.loop(0, CHUNKS)
    def _(j):
        hand_on(j).wait_send()
        half_copy(j).wait_send()

    @pl.when(away)
    def _():
        each_piece(lambda q: bits_copy(q).wait_send())

    @pl.when(home)
    def _():
        @pl.loop(0, 2)
        def _(r):
            each_piece(lambda q: kern_to_x(r, q).wait_send())
            each_piece(lambda q: kern_to_core(x, r, q).wait_send())
            each_piece(lambda q: kern_to_core(1 - x, r, q).wait_send())


def one_kernel(library_bits, library_count, landmark_bits, landmark_count, inverse_root):
    del library_count
    rows, bits = library_bits.shape
    lmks = landmark_bits.shape[0]
    depth, cols = inverse_root.shape
    width = cols // CHUNKS
    hbm = pl.BlockSpec(memory_space=pl.ANY)
    vmem = pl.BlockSpec(memory_space=pltpu.VMEM)
    dma = pltpu.SemaphoreType.DMA
    return pl.pallas_call(
        body,
        out_shape=jax.ShapeDtypeStruct((rows, cols), jnp.float32),
        in_specs=[hbm, hbm, vmem, hbm],
        out_specs=vmem,
        scratch_shapes=[
            pltpu.VMEM((2, rows, bits), jnp.bfloat16),
            pltpu.VMEM((lmks, bits), jnp.bfloat16),
            pltpu.VMEM((2, 2, rows, lmks), jnp.bfloat16),
            pltpu.VMEM((2, 2, CHUNKS, depth, width), jnp.bfloat16),
            pltpu.VMEM((CHUNKS, rows, width), jnp.bfloat16),
            pltpu.VMEM((CHUNKS, rows, width), jnp.bfloat16),
            dma((CHUNKS,)),
            dma((2,)),
            dma((2, PIECES)),
            dma((3, CHUNKS)),
            dma((3, CHUNKS)),
            dma((2, PIECES)),
            dma((2, 2, PIECES)),
            dma((2, 2, PIECES)),
            dma((CHUNKS,)),
            dma((CHUNKS,)),
        ],
        compiler_params=pltpu.CompilerParams(
            collective_id=0, has_side_effects=True, vmem_limit_bytes=60 * 1024 * 1024
        ),
        cost_estimate=pl.CostEstimate(
            flops=2 * rows * (lmks * bits + 4 * lmks * cols),
            bytes_accessed=2 * (rows * bits + lmks * bits + depth * cols) + 4 * rows * cols,
            transcendentals=0,
        ),
    )(library_bits, landmark_bits, landmark_count.reshape(1, lmks), inverse_root)


def solution(mesh):
    placed = (P("lib", None), P("lib"), P("lmk", None), P("lmk"), P("lib", "lmk"))
    n_lib, n_lmk = mesh.shape["lib"], mesh.shape["lmk"]

    def shards(*blocks):
        if (n_lib, n_lmk) == (8, 4):
            return one_kernel(*blocks)
        return split_sum(n_lib, n_lmk, *blocks)

    return jax.shard_map(
        shards, mesh=mesh, in_specs=placed, out_specs=P("lib", "lmk"), check_vma=False
    )
```

```python
import jax
import jax.numpy as jnp
from jax import lax
from jax.experimental import pallas as pl
from jax.experimental.pallas import tpu as pltpu
from jax.sharding import PartitionSpec as P

MESH = pl.DeviceIdType.MESH
CHUNKS = 8
AHEAD_Y, AHEAD_Z = 2, 3
PIECES = 3
EARLY = PIECES + 1

DEPTH = 4


def tversky(row_bits, row_count, col_bits, col_count):
    common = lax.dot_general(
        row_bits, col_bits, (((1,), (1,)), ((), ())), preferred_element_type=jnp.float32
    )
    scale_sum = (
        0.9 * row_count.astype(jnp.float32)[:, None] + 0.1 * col_count.astype(jnp.float32)[None, :]
    )
    return (common / scale_sum).astype(jnp.bfloat16)


def split_sum(n_lib, n_lmk, library_bits, library_count, landmark_bits, landmark_count, inverse_root):
    layer = n_lib // DEPTH
    swap = [(i, i ^ layer) for i in range(n_lib)]
    parity = (lax.axis_index("lib") // layer) % 2
    groups = [[i for i in range(n_lib) if (i // layer) % 2 == p] for p in (0, 1)]
    root = lax.all_gather(inverse_root, "lib", axis=0, tiled=True, axis_index_groups=groups)

    rows = library_bits.shape[0]
    other_bits = lax.ppermute(library_bits, "lib", swap)
    other_count = lax.ppermute(library_count, "lib", swap)
    block = tversky(
        jnp.concatenate([other_bits, library_bits]),
        jnp.concatenate([other_count, library_count]),
        landmark_bits,
        landmark_count,
    )
    kernel = lax.all_gather(block, "lmk", axis=1, tiled=True)
    quarter = kernel.shape[1] // DEPTH
    half = jnp.concatenate(
        [lax.dynamic_slice_in_dim(kernel, (2 * k + parity) * quarter, quarter, 1) for k in (0, 1)], 1
    )
    theirs = jnp.dot(half[:rows], root, preferred_element_type=jnp.float32).astype(jnp.bfloat16)
    arrived = lax.ppermute(theirs, "lib", swap)
    mine = jnp.dot(half[rows:], root, preferred_element_type=jnp.float32)
    return mine + arrived.astype(jnp.float32)


def body(lib_hbm, lmk_hbm, lmk_count, root_hbm, out, lib, lmk, kern, root, sent, came, root_sem,
         load_sem, bits_sem, root_send, root_recv, kern_x, kern_c, kern_recv, half_send, half_recv):
    i, m = lax.axis_index("lib"), lax.axis_index("lmk")
    zh, zl, y = lax.div(i, 4), lax.rem(lax.div(i, 2), 2), lax.rem(i, 2)
    x, core = lax.div(m, 2), lax.rem(m, 2)
    by_y = (i + 1 - 2 * y, m)
    by_zl = (i + 2 - 4 * zl, m)
    by_zh = (i + 4 - 8 * zh, m)
    by_x = (i, m + 2 - 4 * x)
    by_core = (i, m + 1 - 2 * core)
    home = core == zl
    away = core != zl
    rows = lib.shape[1]
    part = rows // PIECES
    width = root.shape[4]

    def columns(j):
        return pl.ds(pl.multiple_of(j * width, width), width)

    def remote(src, dst, send, recv, peer):
        return pltpu.make_async_remote_copy(
            src_ref=src, dst_ref=dst, send_sem=send, recv_sem=recv, device_id=peer, device_id_type=MESH
        )

    def load_root(j):
        return pltpu.make_async_copy(root_hbm.at[:, columns(j)], root.at[zh, y, j], root_sem.at[j])

    def root_copy(way, j, p, q, peer):
        at = root.at[p, q, j]
        return remote(at, at, root_send.at[way, j], root_recv.at[way, j], peer)

    def to_y(j):
        return root_copy(0, j, zh, y, by_y)

    def to_zh(j):
        return root_copy(1, j, zh, y, by_zh)

    def hand_on(j):
        return root_copy(2, j, 1 - zh, y, by_y)

    def piece(q):
        return pl.ds(pl.multiple_of(q * part, part), part)

    def bits_copy(q):
        return remote(
            lib_hbm.at[piece(q)], lib.at[1, piece(q)], bits_sem.at[0, q], bits_sem.at[1, q], by_zl
        )

    def kern_copy(p, r, q, send, peer):
        at = kern.at[p, r, piece(q)]
        return remote(at, at, send, kern_recv.at[p, r, q], peer)

    def kern_to_x(r, q):
        return kern_copy(x, r, q, kern_x.at[r, q], by_x)

    def kern_from_x(r, q):
        return kern_copy(1 - x, r, q, kern_x.at[r, q], by_x)

    def kern_to_core(p, r, q):
        return kern_copy(p, r, q, kern_c.at[p, r, q], by_core)

    def each_piece(step):
        pl.loop(0, PIECES)(step)

    def half_copy(j):
        return remote(
            sent.at[j], came.at[j], half_send.at[j], half_recv.at[j], by_zl
        )

    load_lib = pltpu.make_async_copy(lib_hbm, lib.at[0], load_sem.at[0])
    load_lmk = pltpu.make_async_copy(lmk_hbm, lmk, load_sem.at[1])

    @pl.loop(0, CHUNKS)
    def _(j):
        load_root(j).start()

    @pl.when(home)
    def _():
        load_lib.start()
        load_lmk.start()

    barrier = pltpu.get_barrier_semaphore()
    for peer in (by_y, by_zl, by_zh, by_x, by_core):
        pl.semaphore_signal(barrier, inc=1, device_id=peer, device_id_type=MESH)
    pl.semaphore_wait(barrier, 5)

    @pl.when(away)
    def _():
        each_piece(lambda q: bits_copy(q).start())

    @pl.loop(0, CHUNKS)
    def _(j):
        load_root(j).wait()

        @pl.when(j < AHEAD_Z)
        def _():
            to_zh(j).start()

        @pl.when(j < AHEAD_Y)
        def _():
            to_y(j).start()

    def serve(j):
        to_zh(j).wait_recv()
        hand_on(j).start()

        @pl.when(j + AHEAD_Z < CHUNKS)
        def _():
            to_zh(j).wait_send()
            to_zh(j + AHEAD_Z).start()

        @pl.when(j + AHEAD_Y < CHUNKS)
        def _():
            to_y(j).wait_send()
            to_y(j + AHEAD_Y).start()

    def tversky_piece(r, q):
        ones = jnp.ones((lib.shape[2], 128), jnp.bfloat16)
        row_count = jnp.dot(lib[r, piece(q)], ones, preferred_element_type=jnp.float32)[:, :1]
        step = min(256, lmk.shape[0])

        @pl.loop(0, lmk.shape[0] // step)
        def _(k):
            at = pl.ds(pl.multiple_of(k * step, step), step)
            common = lax.dot_general(
                lib[r, piece(q)],
                lmk[at, :],
                (((1,), (1,)), ((), ())),
                preferred_element_type=jnp.float32,
            )
            scale_sum = 0.9 * row_count + 0.1 * lmk_count[:, at].astype(jnp.float32)
            kern[x, r, piece(q), at] = (common / scale_sum).astype(jnp.bfloat16)

        kern_to_x(r, q).start()
        kern_to_core(x, r, q).start()

    def pass_to_core(r, q):
        kern_from_x(r, q).wait_recv()
        kern_to_core(1 - x, r, q).start()

    @pl.when(home)
    def _():
        load_lib.wait()
        load_lmk.wait()
        each_piece(lambda q: tversky_piece(0, q))

    @pl.loop(0, EARLY)
    def _(j):
        serve(j)

        @pl.when(home & (j < PIECES))
        def _():
            bits_copy(j).wait_recv()
            tversky_piece(1, j)

        @pl.when(home & (j == 1))
        def _():
            each_piece(lambda q: pass_to_core(0, q))

    @pl.when(home)
    def _():
        each_piece(lambda q: pass_to_core(1, q))

    @pl.when(away)
    def _():
        @pl.loop(0, 2)
        def _(r):
            each_piece(lambda q: kern_to_core(x, r, q).wait_recv())
            each_piece(lambda q: kern_to_core(1 - x, r, q).wait_recv())

    def finish(j):
        half_copy(j).wait_recv()
        out[:, columns(j)] += came[j].astype(jnp.float32)

    def half_sum(r, j):
        depth = 2 * root.shape[3]
        return sum(
            jnp.dot(
                kern[p, r],
                root[p, :, j].reshape(depth, width),
                preferred_element_type=jnp.float32,
            )
            for p in (0, 1)
        )

    @pl.loop(0, CHUNKS)
    def _(j):
        @pl.when((j + 1 >= EARLY) & (j + 1 < CHUNKS))
        def _():
            serve(j + 1)

        to_y(j).wait_recv()
        hand_on(j).wait_recv()
        sent[j] = half_sum(1, j).astype(jnp.bfloat16)
        half_copy(j).start()
        out[:, columns(j)] = half_sum(0, j)

        @pl.when(j > 0)
        def _():
            finish(j - 1)

    finish(CHUNKS - 1)

    @pl.loop(CHUNKS - AHEAD_Y, CHUNKS)
    def _(j):
        to_y(j).wait_send()

    @pl.loop(CHUNKS - AHEAD_Z, CHUNKS)
    def _(j):
        to_zh(j).wait_send()

    @pl.loop(0, CHUNKS)
    def _(j):
        hand_on(j).wait_send()
        half_copy(j).wait_send()

    @pl.when(away)
    def _():
        each_piece(lambda q: bits_copy(q).wait_send())

    @pl.when(home)
    def _():
        @pl.loop(0, 2)
        def _(r):
            each_piece(lambda q: kern_to_x(r, q).wait_send())
            each_piece(lambda q: kern_to_core(x, r, q).wait_send())
            each_piece(lambda q: kern_to_core(1 - x, r, q).wait_send())


def one_kernel(library_bits, library_count, landmark_bits, landmark_count, inverse_root):
    del library_count
    rows, bits = library_bits.shape
    lmks = landmark_bits.shape[0]
    depth, cols = inverse_root.shape
    width = cols // CHUNKS
    hbm = pl.BlockSpec(memory_space=pl.ANY)
    vmem = pl.BlockSpec(memory_space=pltpu.VMEM)
    dma = pltpu.SemaphoreType.DMA
    return pl.pallas_call(
        body,
        out_shape=jax.ShapeDtypeStruct((rows, cols), jnp.float32),
        in_specs=[hbm, hbm, vmem, hbm],
        out_specs=vmem,
        scratch_shapes=[
            pltpu.VMEM((2, rows, bits), jnp.bfloat16),
            pltpu.VMEM((lmks, bits), jnp.bfloat16),
            pltpu.VMEM((2, 2, rows, lmks), jnp.bfloat16),
            pltpu.VMEM((2, 2, CHUNKS, depth, width), jnp.bfloat16),
            pltpu.VMEM((CHUNKS, rows, width), jnp.bfloat16),
            pltpu.VMEM((CHUNKS, rows, width), jnp.bfloat16),
            dma((CHUNKS,)),
            dma((2,)),
            dma((2, PIECES)),
            dma((3, CHUNKS)),
            dma((3, CHUNKS)),
            dma((2, PIECES)),
            dma((2, 2, PIECES)),
            dma((2, 2, PIECES)),
            dma((CHUNKS,)),
            dma((CHUNKS,)),
        ],
        compiler_params=pltpu.CompilerParams(
            collective_id=0, has_side_effects=True, vmem_limit_bytes=60 * 1024 * 1024
        ),
        cost_estimate=pl.CostEstimate(
            flops=2 * rows * (lmks * bits + 4 * lmks * cols),
            bytes_accessed=2 * (rows * bits + lmks * bits + depth * cols) + 4 * rows * cols,
            transcendentals=0,
        ),
    )(library_bits, landmark_bits, landmark_count.reshape(1, lmks), inverse_root)


def solution(mesh):
    placed = (P("lib", None), P("lib"), P("lmk", None), P("lmk"), P("lib", "lmk"))
    n_lib, n_lmk = mesh.shape["lib"], mesh.shape["lmk"]

    def shards(*blocks):
        if (n_lib, n_lmk) == (8, 4):
            return one_kernel(*blocks)
        return split_sum(n_lib, n_lmk, *blocks)

    return jax.shard_map(
        shards, mesh=mesh, in_specs=placed, out_specs=P("lib", "lmk"), check_vma=False
    )
```

```python
import jax
import jax.numpy as jnp
from jax import lax
from jax.experimental import pallas as pl
from jax.experimental.pallas import tpu as pltpu
from jax.sharding import PartitionSpec as P

MESH = pl.DeviceIdType.MESH
CHUNKS = 8
AHEAD_Y, AHEAD_Z = 1, 2
PIECES = 3
EARLY = PIECES

DEPTH = 4


def tversky(row_bits, row_count, col_bits, col_count):
    common = lax.dot_general(
        row_bits, col_bits, (((1,), (1,)), ((), ())), preferred_element_type=jnp.float32
    )
    scale_sum = (
        0.9 * row_count.astype(jnp.float32)[:, None] + 0.1 * col_count.astype(jnp.float32)[None, :]
    )
    return (common / scale_sum).astype(jnp.bfloat16)


def split_sum(n_lib, n_lmk, library_bits, library_count, landmark_bits, landmark_count, inverse_root):
    layer = n_lib // DEPTH
    swap = [(i, i ^ layer) for i in range(n_lib)]
    parity = (lax.axis_index("lib") // layer) % 2
    groups = [[i for i in range(n_lib) if (i // layer) % 2 == p] for p in (0, 1)]
    root = lax.all_gather(inverse_root, "lib", axis=0, tiled=True, axis_index_groups=groups)

    rows = library_bits.shape[0]
    other_bits = lax.ppermute(library_bits, "lib", swap)
    other_count = lax.ppermute(library_count, "lib", swap)
    block = tversky(
        jnp.concatenate([other_bits, library_bits]),
        jnp.concatenate([other_count, library_count]),
        landmark_bits,
        landmark_count,
    )
    kernel = lax.all_gather(block, "lmk", axis=1, tiled=True)
    quarter = kernel.shape[1] // DEPTH
    half = jnp.concatenate(
        [lax.dynamic_slice_in_dim(kernel, (2 * k + parity) * quarter, quarter, 1) for k in (0, 1)], 1
    )
    theirs = jnp.dot(half[:rows], root, preferred_element_type=jnp.float32).astype(jnp.bfloat16)
    arrived = lax.ppermute(theirs, "lib", swap)
    mine = jnp.dot(half[rows:], root, preferred_element_type=jnp.float32)
    return mine + arrived.astype(jnp.float32)


def body(lib_hbm, lmk_hbm, lmk_count, root_hbm, out, lib, lmk, kern, root, sent, came, root_sem,
         load_sem, bits_sem, root_send, root_recv, kern_x, kern_c, kern_recv, half_send, half_recv):
    i, m = lax.axis_index("lib"), lax.axis_index("lmk")
    zh, zl, y = lax.div(i, 4), lax.rem(lax.div(i, 2), 2), lax.rem(i, 2)
    x, core = lax.div(m, 2), lax.rem(m, 2)
    by_y = (i + 1 - 2 * y, m)
    by_zl = (i + 2 - 4 * zl, m)
    by_zh = (i + 4 - 8 * zh, m)
    by_x = (i, m + 2 - 4 * x)
    by_core = (i, m + 1 - 2 * core)
    home = core == zl
    away = core != zl
    rows = lib.shape[1]
    part = rows // PIECES
    width = root.shape[4]

    def columns(j):
        return pl.ds(pl.multiple_of(j * width, width), width)

    def remote(src, dst, send, recv, peer):
        return pltpu.make_async_remote_copy(
            src_ref=src, dst_ref=dst, send_sem=send, recv_sem=recv, device_id=peer, device_id_type=MESH
        )

    def load_root(j):
        return pltpu.make_async_copy(root_hbm.at[:, columns(j)], root.at[zh, y, j], root_sem.at[j])

    def root_copy(way, j, p, q, peer):
        at = root.at[p, q, j]
        return remote(at, at, root_send.at[way, j], root_recv.at[way, j], peer)

    def to_y(j):
        return root_copy(0, j, zh, y, by_y)

    def to_zh(j):
        return root_copy(1, j, zh, y, by_zh)

    def hand_on(j):
        return root_copy(2, j, 1 - zh, y, by_y)

    def piece(q):
        return pl.ds(pl.multiple_of(q * part, part), part)

    def bits_copy(q):
        return remote(
            lib_hbm.at[piece(q)], lib.at[1, piece(q)], bits_sem.at[0, q], bits_sem.at[1, q], by_zl
        )

    def kern_copy(p, r, q, send, peer):
        at = kern.at[p, r, piece(q)]
        return remote(at, at, send, kern_recv.at[p, r, q], peer)

    def kern_to_x(r, q):
        return kern_copy(x, r, q, kern_x.at[r, q], by_x)

    def kern_from_x(r, q):
        return kern_copy(1 - x, r, q, kern_x.at[r, q], by_x)

    def kern_to_core(p, r, q):
        return kern_copy(p, r, q, kern_c.at[p, r, q], by_core)

    def each_piece(step):
        pl.loop(0, PIECES)(step)

    def half_copy(j):
        return remote(
            sent.at[j], came.at[j], half_send.at[j], half_recv.at[j], by_zl
        )

    load_lib = pltpu.make_async_copy(lib_hbm, lib.at[0], load_sem.at[0])
    load_lmk = pltpu.make_async_copy(lmk_hbm, lmk, load_sem.at[1])

    @pl.loop(0, CHUNKS)
    def _(j):
        load_root(j).start()

    @pl.when(home)
    def _():
        load_lib.start()
        load_lmk.start()

    barrier = pltpu.get_barrier_semaphore()
    for peer in (by_y, by_zl, by_zh, by_x, by_core):
        pl.semaphore_signal(barrier, inc=1, device_id=peer, device_id_type=MESH)
    pl.semaphore_wait(barrier, 5)

    @pl.when(away)
    def _():
        each_piece(lambda q: bits_copy(q).start())

    @pl.loop(0, CHUNKS)
    def _(j):
        load_root(j).wait()

        @pl.when(j < AHEAD_Z)
        def _():
            to_zh(j).start()

        @pl.when(j < AHEAD_Y)
        def _():
            to_y(j).start()

    def serve(j):
        to_zh(j).wait_recv()
        hand_on(j).start()

        @pl.when(j + AHEAD_Z < CHUNKS)
        def _():
            to_zh(j).wait_send()
            to_zh(j + AHEAD_Z).start()

        @pl.when(j + AHEAD_Y < CHUNKS)
        def _():
            to_y(j).wait_send()
            to_y(j + AHEAD_Y).start()

    def tversky_piece(r, q):
        ones = jnp.ones((lib.shape[2], 128), jnp.bfloat16)
        row_count = jnp.dot(lib[r, piece(q)], ones, preferred_element_type=jnp.float32)[:, :1]
        step = min(256, lmk.shape[0])

        @pl.loop(0, lmk.shape[0] // step)
        def _(k):
            at = pl.ds(pl.multiple_of(k * step, step), step)
            common = lax.dot_general(
                lib[r, piece(q)],
                lmk[at, :],
                (((1,), (1,)), ((), ())),
                preferred_element_type=jnp.float32,
            )
            scale_sum = 0.9 * row_count + 0.1 * lmk_count[:, at].astype(jnp.float32)
            kern[x, r, piece(q), at] = (common / scale_sum).astype(jnp.bfloat16)

        kern_to_x(r, q).start()
        kern_to_core(x, r, q).start()

    def pass_to_core(r, q):
        kern_from_x(r, q).wait_recv()
        kern_to_core(1 - x, r, q).start()

    @pl.when(home)
    def _():
        load_lib.wait()
        load_lmk.wait()
        each_piece(lambda q: tversky_piece(0, q))

    @pl.loop(0, EARLY)
    def _(j):
        serve(j)

        @pl.when(home & (j < PIECES))
        def _():
            bits_copy(j).wait_recv()
            tversky_piece(1, j)

        @pl.when(home & (j == 1))
        def _():
            each_piece(lambda q: pass_to_core(0, q))

    @pl.when(home)
    def _():
        each_piece(lambda q: pass_to_core(1, q))

    @pl.when(away)
    def _():
        @pl.loop(0, 2)
        def _(r):
            each_piece(lambda q: kern_to_core(x, r, q).wait_recv())
            each_piece(lambda q: kern_to_core(1 - x, r, q).wait_recv())

    def finish(j):
        half_copy(j).wait_recv()
        out[:, columns(j)] += came[j].astype(jnp.float32)

    def half_sum(r, j):
        depth = 2 * root.shape[3]
        return sum(
            jnp.dot(
                kern[p, r],
                root[p, :, j].reshape(depth, width),
                preferred_element_type=jnp.float32,
            )
            for p in (0, 1)
        )

    @pl.loop(0, CHUNKS)
    def _(j):
        @pl.when(j >= EARLY)
        def _():
            serve(j)

        to_y(j).wait_recv()
        hand_on(j).wait_recv()
        sent[j] = half_sum(1, j).astype(jnp.bfloat16)
        half_copy(j).start()
        out[:, columns(j)] = half_sum(0, j)

        @pl.when(j > 0)
        def _():
            finish(j - 1)

    finish(CHUNKS - 1)

    @pl.loop(CHUNKS - AHEAD_Y, CHUNKS)
    def _(j):
        to_y(j).wait_send()

    @pl.loop(CHUNKS - AHEAD_Z, CHUNKS)
    def _(j):
        to_zh(j).wait_send()

    @pl.loop(0, CHUNKS)
    def _(j):
        hand_on(j).wait_send()
        half_copy(j).wait_send()

    @pl.when(away)
    def _():
        each_piece(lambda q: bits_copy(q).wait_send())

    @pl.when(home)
    def _():
        @pl.loop(0, 2)
        def _(r):
            each_piece(lambda q: kern_to_x(r, q).wait_send())
            each_piece(lambda q: kern_to_core(x, r, q).wait_send())
            each_piece(lambda q: kern_to_core(1 - x, r, q).wait_send())


def one_kernel(library_bits, library_count, landmark_bits, landmark_count, inverse_root):
    del library_count
    rows, bits = library_bits.shape
    lmks = landmark_bits.shape[0]
    depth, cols = inverse_root.shape
    width = cols // CHUNKS
    hbm = pl.BlockSpec(memory_space=pl.ANY)
    vmem = pl.BlockSpec(memory_space=pltpu.VMEM)
    dma = pltpu.SemaphoreType.DMA
    return pl.pallas_call(
        body,
        out_shape=jax.ShapeDtypeStruct((rows, cols), jnp.float32),
        in_specs=[hbm, hbm, vmem, hbm],
        out_specs=vmem,
        scratch_shapes=[
            pltpu.VMEM((2, rows, bits), jnp.bfloat16),
            pltpu.VMEM((lmks, bits), jnp.bfloat16),
            pltpu.VMEM((2, 2, rows, lmks), jnp.bfloat16),
            pltpu.VMEM((2, 2, CHUNKS, depth, width), jnp.bfloat16),
            pltpu.VMEM((CHUNKS, rows, width), jnp.bfloat16),
            pltpu.VMEM((CHUNKS, rows, width), jnp.bfloat16),
            dma((CHUNKS,)),
            dma((2,)),
            dma((2, PIECES)),
            dma((3, CHUNKS)),
            dma((3, CHUNKS)),
            dma((2, PIECES)),
            dma((2, 2, PIECES)),
            dma((2, 2, PIECES)),
            dma((CHUNKS,)),
            dma((CHUNKS,)),
        ],
        compiler_params=pltpu.CompilerParams(
            collective_id=0, has_side_effects=True, vmem_limit_bytes=60 * 1024 * 1024
        ),
        cost_estimate=pl.CostEstimate(
            flops=2 * rows * (lmks * bits + 4 * lmks * cols),
            bytes_accessed=2 * (rows * bits + lmks * bits + depth * cols) + 4 * rows * cols,
            transcendentals=0,
        ),
    )(library_bits, landmark_bits, landmark_count.reshape(1, lmks), inverse_root)


def solution(mesh):
    placed = (P("lib", None), P("lib"), P("lmk", None), P("lmk"), P("lib", "lmk"))
    n_lib, n_lmk = mesh.shape["lib"], mesh.shape["lmk"]

    def shards(*blocks):
        if (n_lib, n_lmk) == (8, 4):
            return one_kernel(*blocks)
        return split_sum(n_lib, n_lmk, *blocks)

    return jax.shard_map(
        shards, mesh=mesh, in_specs=placed, out_specs=P("lib", "lmk"), check_vma=False
    )
```
